128 devices in a mesh: row: 16 (over z, x_hi, core), col: 8 (over y, x_lo).
Axes of the slice: x: 4 (x_hi: 2, x_lo: 2; x = x_hi * 2 + x_lo), y: 4, z: 4, core: 2. Of those that a mesh axis runs over, the one named last changes fastest.
Arguments:
- blocks: bfloat16 [512, 16, 128, 128], P('row', 'col'), may hold values from -0.8984375 to 0.8984375
- pattern: int32 [512, 16], replicated, may hold values from 0 to 511, as said below
- anchors: int32 [3, 512, 16], replicated, may hold values from 0 to 255, as said below
- basis_x: bfloat16 [16, 128], replicated, may hold values from -0.5 to 0.5
- basis_yz: bfloat16 [128, 256], replicated, may hold values from -0.5 to 0.5
Outputs:
- square: float32 [512, 16, 128, 128], P('row', 'col')
- grid_values: float32 [256, 128, 128], P('row', 'col')
The draws below stay inside these ranges and needn't reach their ends.
Inputs may be any that keep to these rules, and one draw needn't show every extreme that they name: pattern[i,k] = (i + d) mod 512 with -8 <= d <= 8; the 16 columns of a row are distinct. For block row i in group g = i // 32, anchors[0,i,k] = (g * 16 - 16 / 2 + u) mod 256 with 0 <= u <= 16; anchors[1,i,k] <= 112; anchors[2,i,k] <= 112.
All inputs are finite; a program needn't handle non-finite values.
Results may differ from the reference program's by a relative error of at most 0.0041.
Values may be sent and summed in bfloat16 or wider, within the bound.
A program may use at most 128 MiB of HBM per device.

```python
from functools import partial
import jax
import jax.numpy as jnp
from jax import lax

B = 128
K = 16
H = 8
R = 32
PL = 16
GY = 128
GZ = 128
TX = 16
TY = 16
TZ = 16
NBR = 512
NXG = 256


def draw_pattern(key, part):
    key = jax.random.fold_in(key, 11)
    width = 2 * H + 1
    scores = jax.random.randint(key, (NBR, width), 0, 2 ** 20) * width + jnp.arange(width, dtype=jnp.int32)[None, :]
    order = jnp.argsort(scores, axis=1)[:, :K]
    offsets = jnp.arange(width, dtype=jnp.int32) - H
    chosen = offsets[order]
    return ((jnp.arange(NBR, dtype=jnp.int32)[:, None] + chosen) % NBR).astype(jnp.int32)


def draw_anchors(key, part):
    key = jax.random.fold_in(key, 23)
    key_x, key_y, key_z = jax.random.split(key, 3)
    margin = TX // 2
    shifts = jax.random.randint(key_x, (NBR, K), 0, PL + 1)
    shifts = shifts.at[0, 0].set(0).at[0, 1].set(margin).at[0, 2].set(margin - 1)
    groups = jnp.arange(NBR, dtype=jnp.int32) // R
    first = (groups[:, None] * PL - margin + shifts) % NXG
    second = jax.random.randint(key_y, (NBR, K), 0, GY - TY + 1)
    second = second.at[0, 0].set(0).at[0, 1].set(GY - TY)
    third = jax.random.randint(key_z, (NBR, K), 0, GZ - TZ + 1)
    third = third.at[0, 0].set(0).at[0, 1].set(GZ - TZ)
    return jnp.stack([first, second, third]).astype(jnp.int32)


def levels(own_key, dims, pieces, smallest, top_value):
    def one(dim, shards_of):
        heights = jax.random.uniform(jax.random.fold_in(jax.random.fold_in(own_key, 6), dim), (shards_of,), jnp.float32, smallest / len(pieces), top_value / len(pieces))
        return jnp.repeat(jnp.exp(heights), dims[dim] // shards_of).reshape((-1,) + (1,) * (len(dims) - dim - 1))

    loudness = one(*pieces[0])
    for cut in pieces[1:]:
        loudness = loudness * one(*cut)
    return loudness


def noise(rng, dims, scale, limit, cuts=(), kind=jnp.bfloat16):
    values = jax.random.normal(rng, dims, jnp.float32) * scale
    if len(cuts) > 0:
        values = levels(rng, dims, cuts, -0.22, 0.18) * values
    return jnp.clip(values, min=-limit, max=limit).astype(kind)


def setup_inputs(seed: int = 0) -> dict:
    key_of = jax.random.split(jax.random.key(seed), 6)
    return {
        "blocks": noise(key_of[0], (NBR, K, B, B), 0.15, 0.8984375, ((0, 16), (1, 8))),
        "pattern": draw_pattern(jax.random.fold_in(key_of[5], 71), 0),
        "anchors": draw_anchors(jax.random.fold_in(key_of[5], 71), 0),
        "basis_x": noise(key_of[3], (TX, B), B ** -0.5, 0.5),
        "basis_yz": noise(key_of[4], (B, TY * TZ), B ** -0.5, 0.5),
    }


def row_square(blocks, pattern, row_id):
    columns = pattern[row_id]
    gathered = blocks[columns].astype(jnp.float32)
    far_pattern = pattern[columns]
    matches = (far_pattern[:, :, None] == columns[None, None, :]).astype(jnp.float32)
    selected = jnp.einsum('kts,ktmn->ksmn', matches, gathered)
    return jnp.einsum('kmn,ksnp->smp', blocks[row_id].astype(jnp.float32), selected)


def reference(blocks, pattern, anchors, basis_x, basis_yz):
    square = lax.map(partial(row_square, blocks, pattern), jnp.arange(NBR, dtype=jnp.int32))
    density = square.astype(jnp.bfloat16)

    def place(canvas, inputs):
        row_density, row_anchor = inputs
        halves = jnp.einsum('am,kmn->kan', basis_x.astype(jnp.float32), row_density.astype(jnp.float32)).astype(jnp.bfloat16)
        halves = lax.optimization_barrier(halves)
        tile_values = jnp.einsum('kan,nc->kac', halves.astype(jnp.float32), basis_yz.astype(jnp.float32)).reshape(K, TX, TY, TZ)

        def add_one(slot, canvas_now):
            start = (row_anchor[0, slot].astype(jnp.int32), row_anchor[1, slot].astype(jnp.int32), row_anchor[2, slot].astype(jnp.int32))
            current = lax.dynamic_slice(canvas_now, start, (TX, TY, TZ))
            return lax.dynamic_update_slice(canvas_now, current + tile_values[slot], start)

        return lax.fori_loop(0, K, add_one, canvas), None

    canvas_start = jnp.zeros((NXG + TX, GY, GZ), jnp.float32)
    canvas, _ = lax.scan(place, canvas_start, (density, jnp.transpose(anchors, (1, 0, 2))))
    grid_values = canvas[:NXG].at[:TX].add(canvas[NXG:])
    return square, grid_values
```

```python
import functools

import jax
import jax.numpy as jnp
from jax import lax
from jax.experimental import pallas as pl
from jax.experimental.pallas import tpu as pltpu
from jax.sharding import PartitionSpec as P

MESH = pl.DeviceIdType.MESH
B = 128
K = 16
H = 8
UNIT = 4
POS = 5
ROWS = 16
COLS = 8
SHARES = 64
NBR = 512
BLOCKS = POS * UNIT * K
ANY = pl.BlockSpec(memory_space=pl.ANY)
VMEM = pl.BlockSpec(memory_space=pltpu.VMEM)
SMEM = pl.BlockSpec(memory_space=pltpu.SMEM)


def col_of_place(place):
    return place


def place_of_col(col):
    return col


def device_of(share, core):
    share = lax.rem(share + SHARES, SHARES)
    return 2 * (share // 8) + core, col_of_place(lax.rem(share, 8))


def signal(sem, row, col):
    pl.semaphore_signal(sem, inc=1, device_id=(row, col), device_id_type=MESH)


def gather_kernel(blocks, out, send_sem, recv_sem, fwd_send, fwd_recv):
    row = lax.axis_index("row")
    col = lax.axis_index("col")
    core = lax.rem(row, 2)
    share = (row // 2) * 8 + place_of_col(col)
    partner = (row + 1 - 2 * core, col)

    barrier = pltpu.get_barrier_semaphore()
    first_unit = 2 * share - 2 + 3 * core + 128
    row_a = lax.rem(first_unit // 8, ROWS)
    row_b = lax.rem((first_unit + 2) // 8, ROWS)

    @pl.loop(0, COLS)
    def _(c):
        @pl.when(jnp.logical_or(row_a != row, c != col))
        def _():
            signal(barrier, row_a, c)

        @pl.when(jnp.logical_and(row_b != row_a, jnp.logical_or(row_b != row, c != col)))
        def _():
            signal(barrier, row_b, c)

    signal(barrier, *partner)
    place = lax.rem(share, 8)
    is_own = jnp.where(core == 0, place <= 4, place >= 3).astype(jnp.int32)
    pl.semaphore_wait(barrier, 11 - is_own)

    plan = []
    for u in range(8):
        share_u = 4 * row + u // 2
        if u % 2 == 0:
            goals = [(0, -1, 1, 1), (1, 0, 0, 2), (2, 1, 0, 0)]
        else:
            goals = [(0, 0, 1, 0), (1, 1, 0, 1), (2, -1, 1, 2)]
        for t, step, dest_core, j in goals:
            plan.append((t, u, share_u + step, dest_core, j))
    plan.sort(key=lambda item: (item[0], item[1]))

    def copies(t, u, goal, dest_core, j):
        dest_row, dest_col = device_of(goal, dest_core)
        src = blocks.at[pl.ds(UNIT * u, UNIT)]
        dst = out.at[j + 2 * dest_core, col]
        away = pltpu.make_async_remote_copy(
            src_ref=src,
            dst_ref=dst,
            send_sem=send_sem.at[u, t],
            recv_sem=recv_sem.at[j, col],
            device_id=(dest_row, dest_col),
            device_id_type=MESH,
        )
        here = pltpu.make_async_copy(src, dst, recv_sem.at[j, col])
        is_here = jnp.logical_and(dest_row == row, dest_col == col)
        return away, here, is_here

    for item in plan:
        away, here, is_here = copies(*item)

        @pl.when(is_here)
        def _():
            here.start()

        @pl.when(jnp.logical_not(is_here))
        def _():
            away.start()

    def wait_for(j, c):
        slot = out.at[j + 2 * core, c]
        pltpu.make_async_copy(slot, slot, recv_sem.at[j, c]).wait()

    def forward(f, c):
        return pltpu.make_async_remote_copy(
            src_ref=out.at[1 + core + f, c],
            dst_ref=out.at[3 * core + f, c],
            send_sem=fwd_send.at[f, c],
            recv_sem=fwd_recv.at[f, c],
            device_id=partner,
            device_id_type=MESH,
        )

    for f in range(2):

        @pl.loop(0, COLS)
        def _(c):
            wait_for(f + 1 - core, c)
            forward(f, c).start()

    @pl.loop(0, COLS)
    def _(c):
        wait_for(2 * core, c)

    for f in range(2):

        @pl.loop(0, COLS)
        def _(c):
            forward(f, c).wait()

    for item in plan:
        away, here, is_here = copies(*item)

        @pl.when(jnp.logical_not(is_here))
        def _():
            away.wait_send()


def gather(blocks):
    return pl.pallas_call(
        gather_kernel,
        out_shape=jax.ShapeDtypeStruct((POS, COLS, UNIT, 2, B, B), jnp.bfloat16),
        in_specs=[ANY],
        out_specs=ANY,
        scratch_shapes=[
            pltpu.SemaphoreType.DMA((8, 3)),
            pltpu.SemaphoreType.DMA((3, COLS)),
            pltpu.SemaphoreType.DMA((2, COLS)),
            pltpu.SemaphoreType.DMA((2, COLS)),
        ],
        compiler_params=pltpu.CompilerParams(collective_id=0, has_side_effects=True),
        name="gather_rows",
    )(blocks)


def square_kernel(
    index, corners, blocks, planes, cells, density, mid, low, high, held, halves, tiles, slab, sem
):
    load = pltpu.make_async_copy(blocks, held.at[pl.ds(0, BLOCKS)], sem)
    load.start()
    held[BLOCKS] = jnp.zeros((B, B), jnp.bfloat16)

    @pl.loop(0, 128)
    def _(y):
        slab[y] = jnp.zeros((32, 128), jnp.float32)

    load.wait()

    @pl.loop(0, UNIT)
    def _(i):
        @pl.loop(0, K // 2)
        def _(pair):
            total = jnp.zeros((B, 2 * B), jnp.float32)
            for kk in range(K // 2):
                first = (2 * COLS + kk) * 2 * UNIT + 2 * i
                left = jnp.concatenate([held[first], held[first + 1]], axis=1)
                at = (i * K + 2 * pair) * K + 2 * kk
                right = jnp.concatenate(
                    [
                        jnp.concatenate([held[index[at]], held[index[at + K]]], axis=1),
                        jnp.concatenate([held[index[at + 1]], held[index[at + K + 1]]], axis=1),
                    ],
                    axis=0,
                )
                total += jnp.dot(left, right, preferred_element_type=jnp.float32)
            rounded = total.astype(jnp.bfloat16)
            for e in range(2):
                block = rounded[:, e * B : (e + 1) * B]
                density[pair, i, e] = block
                tile = 2 * pair + e
                placed = pltpu.roll(planes[...], corners[i * K + tile], 0).astype(jnp.bfloat16)
                half = jnp.dot(placed, block, preferred_element_type=jnp.float32)
                halves[pl.ds(pl.multiple_of(tile * 32, 32), 32), :] = half.astype(jnp.bfloat16)

        for b in range(0, 16, 2):
            tiles[:, b * 128 : (b + 2) * 128] = jnp.dot(
                halves[...], cells[:, b * 128 : (b + 2) * 128], preferred_element_type=jnp.float32
            )

        @pl.loop(0, K)
        def _(tile):
            y = corners[UNIT * K + i * K + tile]
            z = corners[2 * UNIT * K + i * K + tile]
            rows = pl.ds(pl.multiple_of(tile * 32, 32), 32)
            for b in range(16):
                slab[y + b] += pltpu.roll(tiles[rows, b * 128 : (b + 1) * 128], z, 1)

    @pl.loop(0, 64)
    def _(y):
        for e in range(2):
            mid[2 * y + e] = slab[2 * y + e, 8:24, :].astype(jnp.bfloat16)
        low[y] = jnp.concatenate([slab[2 * y, 0:8, :], slab[2 * y + 1, 0:8, :]], axis=0).astype(jnp.bfloat16)
        high[y] = jnp.concatenate([slab[2 * y, 24:32, :], slab[2 * y + 1, 24:32, :]], axis=0).astype(
            jnp.bfloat16
        )


def square_rows(index, corners, blocks, planes, cells):
    return pl.pallas_call(
        square_kernel,
        out_shape=[
            jax.ShapeDtypeStruct((COLS, UNIT, 2, B, B), jnp.bfloat16),
            jax.ShapeDtypeStruct((128, 16, 128), jnp.bfloat16),
            jax.ShapeDtypeStruct((64, 16, 128), jnp.bfloat16),
            jax.ShapeDtypeStruct((64, 16, 128), jnp.bfloat16),
        ],
        in_specs=[SMEM, SMEM, ANY, VMEM, VMEM],
        out_specs=[VMEM] * 4,
        scratch_shapes=[
            pltpu.VMEM((BLOCKS + 1, B, B), jnp.bfloat16),
            pltpu.VMEM((K * 32, B), jnp.bfloat16),
            pltpu.VMEM((K * 32, 16 * 128), jnp.float32),
            pltpu.VMEM((128, 32, 128), jnp.float32),
            pltpu.SemaphoreType.DMA,
        ],
        compiler_params=pltpu.CompilerParams(vmem_limit_bytes=48 << 20),
        name="square_rows",
    )(index, corners, blocks, planes, cells)


def return_kernel(density, mid, low, high, square, own, below, above, send_sem, recv_sem):
    row = lax.axis_index("row")
    col = lax.axis_index("col")
    core = lax.rem(row, 2)
    unit = 2 * ((row // 2) * 8 + place_of_col(col)) + core
    owner = unit // 8
    u = lax.rem(unit, 8)
    up = lax.rem(owner + 1, ROWS)
    down = lax.rem(owner + ROWS - 1, ROWS)

    barrier = pltpu.get_barrier_semaphore()

    @pl.loop(0, 24)
    def _(v):
        n = 8 * (row - 1) + v + 128
        from_row, from_col = device_of(n // 2, lax.rem(n, 2))

        @pl.when(jnp.logical_or(from_row != row, from_col != col))
        def _():
            signal(barrier, from_row, from_col)

    pl.semaphore_wait(barrier, 23)

    def pieces(c):
        kinds = [
            (density.at[c], square.at[pl.ds(UNIT * u, UNIT)], owner),
            (mid.at[pl.ds(16 * c, 16)], own.at[u], owner),
            (low.at[pl.ds(8 * c, 8)], above.at[u], down),
            (high.at[pl.ds(8 * c, 8)], below.at[u], up),
        ]
        for kind, (src, dst, to_row) in enumerate(kinds):
            away = pltpu.make_async_remote_copy(
                src_ref=src,
                dst_ref=dst,
                send_sem=send_sem.at[kind, c],
                recv_sem=recv_sem.at[kind, u],
                device_id=(to_row, c),
                device_id_type=MESH,
            )
            here = pltpu.make_async_copy(src, dst, recv_sem.at[kind, u])
            yield away, here, jnp.logical_and(to_row == row, c == col)

    @pl.loop(0, COLS)
    def _(step):
        for away, here, is_here in pieces(lax.rem(col + step, COLS)):

            @pl.when(is_here)
            def _():
                here.start()

            @pl.when(jnp.logical_not(is_here))
            def _():
                away.start()

    @pl.loop(0, 8)
    def _(v):
        for kind, ref in enumerate((square.at[pl.ds(UNIT * v, UNIT)], own.at[v], above.at[v], below.at[v])):
            pltpu.make_async_copy(ref, ref, recv_sem.at[kind, v]).wait()

    @pl.loop(0, COLS)
    def _(step):
        for away, here, is_here in pieces(lax.rem(col + step, COLS)):

            @pl.when(jnp.logical_not(is_here))
            def _():
                away.wait_send()


def give_back(density, mid, low, high):
    return pl.pallas_call(
        return_kernel,
        out_shape=[
            jax.ShapeDtypeStruct((32, 2, B, B), jnp.bfloat16),
            jax.ShapeDtypeStruct((8, 16, 16, 128), jnp.bfloat16),
            jax.ShapeDtypeStruct((8, 8, 16, 128), jnp.bfloat16),
            jax.ShapeDtypeStruct((8, 8, 16, 128), jnp.bfloat16),
        ],
        in_specs=[ANY] * 4,
        out_specs=[ANY] * 4,
        scratch_shapes=[pltpu.SemaphoreType.DMA((4, COLS)), pltpu.SemaphoreType.DMA((4, 8))],
        compiler_params=pltpu.CompilerParams(collective_id=1, has_side_effects=True),
        name="give_back",
    )(density, mid, low, high)


def tables(pattern, anchors, unit):
    first = UNIT * unit
    around = jnp.concatenate([pattern[NBR - H :], pattern, pattern[: UNIT + H]], axis=0)
    window = lax.dynamic_slice_in_dim(around, first, UNIT + 2 * H, 0)
    columns = window[H : H + UNIT]
    rel = jnp.arange(UNIT + 2 * H, dtype=jnp.int32)
    row_ids = (first - H + rel + NBR) % NBR
    slots = jnp.arange(K, dtype=jnp.int32)
    places = ((rel[:, None] // 4) * 8 + slots[None, :] // 2) * 8 + (rel[:, None] % 4) * 2 + slots[None, :] % 2
    found = jnp.sum(
        jnp.where(window[None, None] == columns[:, :, None, None], places[None, None] + 1, 0), axis=3
    )
    is_row = columns[:, :, None] == row_ids[None, None, :]
    index = jnp.sum(jnp.where(is_row[:, None, :, :], found[:, :, None, :], 0), axis=3)
    index = jnp.where(index == 0, BLOCKS, index - 1)
    corner = lax.dynamic_slice(anchors, (0, first, 0), (3, UNIT, K))
    group = unit // 8
    planes = (corner[0] - 16 * group + 8 + 256) % 256
    corners = jnp.concatenate([planes[None], corner[1:]], axis=0)
    return index.reshape(-1), corners.reshape(-1)


def per_device(blocks, pattern, anchors, basis_x, basis_yz):
    row = lax.axis_index("row")
    col = lax.axis_index("col")
    unit = 2 * ((row // 2) * 8 + place_of_col(col)) + row % 2
    index, corners = tables(pattern, anchors, unit)
    planes = jnp.concatenate([basis_x, jnp.zeros_like(basis_x)], axis=0).astype(jnp.float32)
    cells = jnp.pad(basis_yz.reshape(B, 16, 16), ((0, 0), (0, 0), (0, 112))).reshape(B, 16 * 128)
    gathered = gather(blocks).reshape(BLOCKS, B, B)
    density, mid, low, high = square_rows(index, corners, gathered, planes, cells)
    square, own, below, above = give_back(density, mid, low, high)
    total = jnp.sum(own.astype(jnp.float32), axis=0)
    low_sum = jnp.sum(below.astype(jnp.float32), axis=0).reshape(16, 8, 128)
    high_sum = jnp.sum(above.astype(jnp.float32), axis=0).reshape(16, 8, 128)
    total = total + jnp.concatenate([low_sum, high_sum], axis=1)
    return square.astype(jnp.float32), jnp.transpose(total, (1, 0, 2))


def solution(mesh):
    placed = (P("row", "col", None, None), P(), P(), P(), P())
    return jax.shard_map(
        per_device,
        mesh=mesh,
        in_specs=placed,
        out_specs=(P("row", "col", None, None), P("row", "col", None)),
        check_vma=False,
    )
```

```python
import jax
import jax.numpy as jnp
import numpy as np
from jax import lax
from jax.experimental import pallas as pl
from jax.experimental.pallas import tpu as pltpu
from jax.sharding import PartitionSpec as P

MESH = pl.DeviceIdType.MESH
B = 128
K = 16
H = 8
UNIT = 4
ROWS = 16
COLS = 8
SHARES = 64
NBR = 512
HELD = UNIT * K
ORDER = ((2, 1, 3, 4, 0), (2, 3, 1, 0, 4))
LEFT = 5 * UNIT * UNIT * K
ANY = pl.BlockSpec(memory_space=pl.ANY)
VMEM = pl.BlockSpec(memory_space=pltpu.VMEM)
SMEM = pl.BlockSpec(memory_space=pltpu.SMEM)


def col_of_place(place):
    return place


def place_of_col(col):
    return col


def device_of(share, core):
    share = lax.rem(share + SHARES, SHARES)
    return 2 * (share // 8) + core, col_of_place(lax.rem(share, 8))


def signal(sem, row, col):
    pl.semaphore_signal(sem, inc=1, device_id=(row, col), device_id_type=MESH)


def kernel(
    index, corners, blocks, planes, cells,
    square, grid,
    held0, held1, held2, held3, held4, sums, density, halves, tiles, mid, low, high, own, below, above, total,
    send_sem, recv_sem, fwd_send, fwd_recv, back_send, back_recv,
):
    row = lax.axis_index("row")
    col = lax.axis_index("col")
    core = lax.rem(row, 2)
    share = (row // 2) * 8 + place_of_col(col)
    partner = (row + 1 - 2 * core, col)
    unit = 2 * share + core
    owner = unit // 8
    u_back = lax.rem(unit, 8)
    up = lax.rem(owner + 1, ROWS)
    down = lax.rem(owner + ROWS - 1, ROWS)
    held = (held0, held1, held2, held3, held4)

    for ref in held:
        ref[HELD] = jnp.zeros((B, B), jnp.bfloat16)
    tiles[1024] = jnp.zeros((32, B), jnp.float32)

    barrier = pltpu.get_barrier_semaphore()
    first_unit = 2 * share - 2 + 3 * core + 128
    row_a = lax.rem(first_unit // 8, ROWS)
    row_b = lax.rem((first_unit + 2) // 8, ROWS)

    @pl.loop(0, COLS)
    def _(c):
        @pl.when(jnp.logical_or(row_a != row, c != col))
        def _():
            signal(barrier, row_a, c)

        @pl.when(jnp.logical_and(row_b != row_a, jnp.logical_or(row_b != row, c != col)))
        def _():
            signal(barrier, row_b, c)

    @pl.loop(0, 24)
    def _(v):
        n = 8 * (row - 1) + v + 128
        from_row, from_col = device_of(n // 2, lax.rem(n, 2))

        @pl.when(jnp.logical_or(from_row != row, from_col != col))
        def _():
            signal(barrier, from_row, from_col)

    signal(barrier, *partner)
    place = lax.rem(share, 8)
    is_own = jnp.where(core == 0, place <= 4, place >= 3).astype(jnp.int32)
    pl.semaphore_wait(barrier, 34 - is_own)

    plan = ((0, 1, 0, 1), (0, 0, 0, 0), (1, 0, -1, 1), (1, 1, 1, 0), (2, 0, 1, 0), (2, 1, -1, 1))

    def sends(v, kind, parity, step, goal_core):
        u = 2 * v + parity
        goal_row, goal_col = device_of(4 * row + v + step, goal_core)
        src = blocks.at[pl.ds(2 * UNIT * u, 2 * UNIT)]
        dst = held[4 if kind == 2 else kind].at[pl.ds(2 * UNIT * col, 2 * UNIT)]
        away = pltpu.make_async_remote_copy(
            src_ref=src,
            dst_ref=dst,
            send_sem=send_sem.at[u, kind],
            recv_sem=recv_sem.at[kind, col],
            device_id=(goal_row, goal_col),
            device_id_type=MESH,
        )
        is_here = jnp.logical_and(goal_row == row, goal_col == col)
        return src, dst, recv_sem.at[kind, col], away, is_here

    for half in range(3):

        @pl.loop(0, 4)
        def _(w):
            v = lax.rem(w + col, 4)
            for item in plan[2 * half : 2 * half + 2]:
                src, dst, sem, away, is_here = sends(v, *item)

                @pl.when(is_here)
                def _():
                    pltpu.make_async_copy(src, dst, sem).start()

                @pl.when(jnp.logical_not(is_here))
                def _():
                    away.start()

    def part(ref, c):
        return ref.at[pl.ds(2 * UNIT * c, 2 * UNIT)]

    def forward(f, c):
        return pltpu.make_async_remote_copy(
            src_ref=part(held[f], c),
            dst_ref=part(held[2 + f], c),
            send_sem=fwd_send.at[f, c],
            recv_sem=fwd_recv.at[f, c],
            device_id=partner,
            device_id_type=MESH,
        )

    def wait_for(kind, c):
        slot = part(held[4 if kind == 2 else kind], c)
        pltpu.make_async_copy(slot, slot, recv_sem.at[kind, c]).wait()

    for f in range(2):

        @pl.loop(0, COLS)
        def _(c):
            wait_for(f, c)
            forward(f, c).start()

    def product(rank, i, pair):
        out = jnp.zeros((B, 2 * B), jnp.float32)
        for kk in range(0, UNIT, 2):
            lefts = [held0[index[LEFT + (rank * UNIT + kk + e) * UNIT + i]] for e in range(2)]
            rights = []
            for e in range(2):
                at = ((rank * UNIT + kk + e) * UNIT + i) * K + 2 * pair
                rights.append(jnp.concatenate([held[rank][index[at]], held[rank][index[at + 1]]], axis=1))
            out += jnp.dot(
                jnp.concatenate(lefts, axis=1), jnp.concatenate(rights, axis=0), preferred_element_type=jnp.float32
            )
        return out

    for rank in range(4):
        if rank >= 2:

            @pl.loop(0, COLS)
            def _(c):
                forward(rank - 2, c).wait()

        @pl.loop(0, UNIT * K // 2)
        def _(at):
            value = product(rank, at // (K // 2), lax.rem(at, K // 2))
            sums[at] = value if rank == 0 else sums[at] + value

    @pl.loop(0, COLS)
    def _(c):
        wait_for(2, c)

    def goes_back(kind, c):
        src, dst, to_row = (
            (density.at[pl.ds(2 * UNIT * c, 2 * UNIT)], square.at[pl.ds(2 * UNIT * u_back, 2 * UNIT)], owner),
            (mid.at[pl.ds(16 * c, 16)], own.at[u_back], owner),
            (low.at[pl.ds(8 * c, 8)], above.at[u_back], down),
            (high.at[pl.ds(8 * c, 8)], below.at[u_back], up),
        )[kind]
        away = pltpu.make_async_remote_copy(
            src_ref=src,
            dst_ref=dst,
            send_sem=back_send.at[kind, c],
            recv_sem=back_recv.at[kind, u_back],
            device_id=(to_row, c),
            device_id_type=MESH,
        )
        return src, dst, back_recv.at[kind, u_back], away, jnp.logical_and(to_row == row, c == col)

    def start_back(kind, c):
        src, dst, sem, away, is_here = goes_back(kind, c)

        @pl.when(is_here)
        def _():
            pltpu.make_async_copy(src, dst, sem).start()

        @pl.when(jnp.logical_not(is_here))
        def _():
            away.start()

    @pl.loop(0, COLS)
    def _(w):
        pair = lax.rem(w + col, COLS)

        @pl.loop(0, UNIT)
        def _(i):
            value = (sums[i * (K // 2) + pair] + product(4, i, pair)).astype(jnp.bfloat16)
            for e in range(2):
                density[2 * UNIT * pair + 2 * i + e] = value[:, e * B : (e + 1) * B]

        start_back(0, pair)

    @pl.loop(0, UNIT)
    def _(i):
        @pl.loop(0, K // 2)
        def _(pair):
            for e in range(2):
                tile = 2 * pair + e
                placed = pltpu.roll(planes[...], corners[i * K + tile], 0).astype(jnp.bfloat16)
                half = jnp.dot(placed, density[2 * UNIT * pair + 2 * i + e], preferred_element_type=jnp.float32)
                halves[pl.ds(pl.multiple_of(tile * 32, 32), 32), :] = half.astype(jnp.bfloat16)

        @pl.loop(0, K // 4)
        def _(four):
            rows = pl.ds(pl.multiple_of(four * 128, 128), 128)
            shifts = [corners[2 * UNIT * K + i * K + 4 * four + e] for e in range(4)]
            for b in range(0, 16, 2):
                values = jnp.dot(
                    halves[rows, :], cells[:, b * 128 : (b + 2) * 128], preferred_element_type=jnp.float32
                )
                for e in range(4):
                    for f in range(2):
                        piece = values[e * 32 : (e + 1) * 32, f * 128 : (f + 1) * 128]
                        tiles[(i * K + 4 * four + e) * 16 + b + f] = pltpu.roll(piece, shifts[e], 1)

    def plane_sum(y):
        value = jnp.zeros((32, B), jnp.float32)
        for tile in range(UNIT * K):
            off = y - corners[UNIT * K + tile]
            inside = jnp.logical_and(off >= 0, off < 16)
            value += tiles[jnp.where(inside, tile * 16 + off, 1024)]
        return value

    @pl.loop(0, COLS)
    def _(w):
        c = lax.rem(w + col, COLS)

        @pl.loop(0, 8)
        def _(yy):
            at = 8 * c + yy
            both = [plane_sum(2 * at + e) for e in range(2)]
            for e in range(2):
                mid[2 * at + e] = both[e][8:24].astype(jnp.bfloat16)
            low[at] = jnp.concatenate([both[0][0:8], both[1][0:8]], axis=0).astype(jnp.bfloat16)
            high[at] = jnp.concatenate([both[0][24:32], both[1][24:32]], axis=0).astype(jnp.bfloat16)

        for kind in (1, 2, 3):
            start_back(kind, c)

    @pl.loop(0, 8)
    def _(v):
        refs = (square.at[pl.ds(2 * UNIT * v, 2 * UNIT)], own.at[v], above.at[v], below.at[v])
        for kind, ref in enumerate(refs):
            pltpu.make_async_copy(ref, ref, back_recv.at[kind, v]).wait()

    def added(ref, at):
        value = ref[0, at].astype(jnp.float32)
        for v in range(1, 8):
            value += ref[v, at].astype(jnp.float32)
        return value

    @pl.loop(0, 8)
    def _(yy):
        under, over = added(below, yy), added(above, yy)
        for e in range(2):
            rims = jnp.concatenate([under[8 * e : 8 * e + 8], over[8 * e : 8 * e + 8]], axis=0)
            at = pl.multiple_of((2 * yy + e) * 16, 16)
            total[pl.ds(at, 16), :] = added(own, 2 * yy + e) + rims

    for x in range(16):
        grid[x] = total[pl.ds(x, 16, stride=16), :]

    @pl.loop(0, 4)
    def _(v):
        for item in plan:
            away, is_here = sends(v, *item)[3:]

            @pl.when(jnp.logical_not(is_here))
            def _():
                away.wait_send()

    @pl.loop(0, COLS)
    def _(c):
        for kind in range(4):
            away, is_here = goes_back(kind, c)[3:]

            @pl.when(jnp.logical_not(is_here))
            def _():
                away.wait_send()


def fused(index, corners, blocks, planes, cells):
    return pl.pallas_call(
        kernel,
        out_shape=[
            jax.ShapeDtypeStruct((64, B, B), jnp.bfloat16),
            jax.ShapeDtypeStruct((16, 16, 128), jnp.float32),
        ],
        in_specs=[SMEM, SMEM, ANY, VMEM, VMEM],
        out_specs=[ANY, VMEM],
        scratch_shapes=[pltpu.VMEM((HELD + 1, B, B), jnp.bfloat16)] * 5
        + [
            pltpu.VMEM((UNIT * K // 2, B, 2 * B), jnp.float32),
            pltpu.VMEM((HELD, B, B), jnp.bfloat16),
            pltpu.VMEM((K * 32, B), jnp.bfloat16),
            pltpu.VMEM((1025, 32, 128), jnp.float32),
            pltpu.VMEM((128, 16, 128), jnp.bfloat16),
            pltpu.VMEM((64, 16, 128), jnp.bfloat16),
            pltpu.VMEM((64, 16, 128), jnp.bfloat16),
            pltpu.VMEM((8, 16, 16, 128), jnp.bfloat16),
            pltpu.VMEM((8, 8, 16, 128), jnp.bfloat16),
            pltpu.VMEM((8, 8, 16, 128), jnp.bfloat16),
            pltpu.VMEM((256, 128), jnp.float32),
            pltpu.SemaphoreType.DMA((8, 3)),
            pltpu.SemaphoreType.DMA((3, COLS)),
            pltpu.SemaphoreType.DMA((2, COLS)),
            pltpu.SemaphoreType.DMA((2, COLS)),
            pltpu.SemaphoreType.DMA((4, COLS)),
            pltpu.SemaphoreType.DMA((4, 8)),
        ],
        compiler_params=pltpu.CompilerParams(collective_id=0, has_side_effects=True, vmem_limit_bytes=52 << 20),
        name="square_and_tiles",
    )(index, corners, blocks, planes, cells)


def tables(pattern, anchors, unit):
    first = UNIT * unit
    around = jnp.concatenate([pattern[NBR - H :], pattern, pattern[: UNIT + H]], axis=0)
    window = lax.dynamic_slice_in_dim(around, first, UNIT + 2 * H, 0)
    columns = window[H : H + UNIT]
    picks = [np.concatenate([np.arange(UNIT) + UNIT * pos for pos in order]) for order in ORDER]
    on_first = unit % 2 == 0
    far = jnp.where(on_first, window[picks[0]], window[picks[1]])
    far_ids = (first - H + jnp.where(on_first, picks[0], picks[1]) + NBR) % NBR
    slots = jnp.arange(K, dtype=jnp.int32)
    inner = jnp.arange(5 * UNIT, dtype=jnp.int32) % UNIT
    place = (slots // 2) * 8 + slots % 2 + 1
    right = jnp.sum(
        jnp.where(
            far[:, None, None, :] == columns[None, :, :, None], (place + 2 * inner[:, None])[:, None, None, :], 0
        ),
        axis=3,
    )
    rows = jnp.arange(UNIT, dtype=jnp.int32)
    left = jnp.sum(
        jnp.where(columns[None] == far_ids[:, None, None], (place + 2 * rows[:, None])[None], 0), axis=2
    )
    index = jnp.concatenate([right.reshape(-1), left.reshape(-1)])
    index = jnp.where(index == 0, HELD, index - 1)
    corner = lax.dynamic_slice(anchors, (0, first, 0), (3, UNIT, K))
    planes = (corner[0] - 16 * (unit // 8) + 8 + 256) % 256
    corners = jnp.concatenate([planes[None], corner[1:]], axis=0)
    return index, corners.reshape(-1)


def per_device(blocks, pattern, anchors, basis_x, basis_yz):
    row = lax.axis_index("row")
    col = lax.axis_index("col")
    unit = 2 * ((row // 2) * 8 + place_of_col(col)) + row % 2
    index, corners = tables(pattern, anchors, unit)
    planes = jnp.concatenate([basis_x, jnp.zeros_like(basis_x)], axis=0).astype(jnp.float32)
    cells = jnp.pad(basis_yz.reshape(B, 16, 16), ((0, 0), (0, 0), (0, 112))).reshape(B, 16 * 128)
    square, grid = fused(index, corners, blocks.reshape(64, B, B), planes, cells)
    return square.reshape(32, 2, B, B).astype(jnp.float32), grid


def solution(mesh):
    placed = (P("row", "col", None, None), P(), P(), P(), P())
    return jax.shard_map(
        per_device,
        mesh=mesh,
        in_specs=placed,
        out_specs=(P("row", "col", None, None), P("row", "col", None)),
        check_vma=False,
    )
```

```python
import jax
import jax.numpy as jnp
from jax import lax
from jax.experimental import pallas as pl
from jax.experimental.pallas import tpu as pltpu
from jax.sharding import PartitionSpec as P

MESH = pl.DeviceIdType.MESH
B = 128
K = 16
H = 8
UNIT = 4
ROWS = 16
COLS = 8
SHARES = 64
NBR = 512
HELD = UNIT * K
CORNERS = 5 * UNIT * UNIT
TABLE = 96
PAD = 8
SPAN = 32
ANY = pl.BlockSpec(memory_space=pl.ANY)
VMEM = pl.BlockSpec(memory_space=pltpu.VMEM)
SMEM = pl.BlockSpec(memory_space=pltpu.SMEM)


def col_of_place(place):
    return place


def place_of_col(col):
    return col


def device_of(share, core):
    share = lax.rem(share + SHARES, SHARES)
    return 2 * (share // 8) + core, col_of_place(lax.rem(share, 8))


def signal(sem, row, col):
    pl.semaphore_signal(sem, inc=1, device_id=(row, col), device_id_type=MESH)


def kernel(
    pattern, anchors, blocks, basis_x, basis_yz,
    square, grid,
    held0, held1, held2, held3, held4, sums, density, halves, tiles, mid, low, high, own, below, above, total,
    rows_held, corners_held, planes, cells, drawn, index,
    send_sem, recv_sem, fwd_send, fwd_recv, back_send, back_recv, table_sem,
):
    row = lax.axis_index("row")
    col = lax.axis_index("col")
    core = lax.rem(row, 2)
    share = (row // 2) * 8 + place_of_col(col)
    partner = (row + 1 - 2 * core, col)
    unit = 2 * share + core
    owner = unit // 8
    u_back = lax.rem(unit, 8)
    up = lax.rem(owner + 1, ROWS)
    down = lax.rem(owner + ROWS - 1, ROWS)
    held = (held0, held1, held2, held3, held4)

    barrier = pltpu.get_barrier_semaphore()
    first_unit = 2 * share - 2 + 3 * core + 128
    row_a = lax.rem(first_unit // 8, ROWS)
    row_b = lax.rem((first_unit + 2) // 8, ROWS)

    @pl.loop(0, COLS)
    def _(c):
        @pl.when(jnp.logical_or(row_a != row, c != col))
        def _():
            signal(barrier, row_a, c)

        @pl.when(jnp.logical_and(row_b != row_a, jnp.logical_or(row_b != row, c != col)))
        def _():
            signal(barrier, row_b, c)

    @pl.loop(0, 24)
    def _(v):
        n = 8 * (row - 1) + v + 128
        from_row, from_col = device_of(n // 2, lax.rem(n, 2))

        @pl.when(jnp.logical_or(from_row != row, from_col != col))
        def _():
            signal(barrier, from_row, from_col)

    signal(barrier, *partner)
    place = lax.rem(share, 8)
    is_own = jnp.where(core == 0, place <= 4, place >= 3).astype(jnp.int32)
    pl.semaphore_wait(barrier, 34 - is_own)

    plan = ((0, 1, 0, 1), (0, 0, 0, 0), (1, 0, -1, 1), (1, 1, 1, 0), (2, 0, 1, 0), (2, 1, -1, 1))

    def sends(v, kind, parity, step, goal_core):
        u = 2 * v + parity
        goal_row, goal_col = device_of(4 * row + v + step, goal_core)
        src = blocks.at[pl.ds(2 * UNIT * u, 2 * UNIT)]
        dst = held[4 if kind == 2 else kind].at[pl.ds(2 * UNIT * col, 2 * UNIT)]
        away = pltpu.make_async_remote_copy(
            src_ref=src,
            dst_ref=dst,
            send_sem=send_sem.at[u, kind],
            recv_sem=recv_sem.at[kind, col],
            device_id=(goal_row, goal_col),
            device_id_type=MESH,
        )
        is_here = jnp.logical_and(goal_row == row, goal_col == col)
        return src, dst, recv_sem.at[kind, col], away, is_here

    for half in range(3):

        @pl.loop(0, 4)
        def _(w):
            v = lax.rem(w + col // 2, 4)
            for item in plan[2 * half : 2 * half + 2]:
                src, dst, sem, away, is_here = sends(v, *item)

                @pl.when(is_here)
                def _():
                    pltpu.make_async_copy(src, dst, sem).start()

                @pl.when(jnp.logical_not(is_here))
                def _():
                    away.start()

    loads = (
        pltpu.make_async_copy(pattern, rows_held, table_sem.at[0]),
        pltpu.make_async_copy(anchors, corners_held, table_sem.at[1]),
    )
    for load in loads:
        load.start()
    for ref in held:
        ref[HELD] = jnp.zeros((B, B), jnp.bfloat16)

    planes[...] = jnp.concatenate([basis_x[...].astype(jnp.float32), jnp.zeros((16, B), jnp.float32)], axis=0)
    lane = lax.broadcasted_iota(jnp.int32, (B, B), 1)
    for b in range(16):
        half = basis_yz[:, (b // 8) * B : (b // 8 + 1) * B].astype(jnp.float32)
        turned = pltpu.roll(half, (B - 16 * (b % 8)) % B, 1)
        cells[:, b * B : (b + 1) * B] = jnp.where(lane < 16, turned, 0.0).astype(jnp.bfloat16)

    @pl.loop(0, UNIT * K)
    def _(tile):
        for e in range(PAD):
            tiles[tile * SPAN + e] = jnp.zeros((32, B), jnp.float32)
            tiles[tile * SPAN + PAD + 16 + e] = jnp.zeros((32, B), jnp.float32)

    for load in loads:
        load.wait()
    columns = rows_held[pl.ds(UNIT * unit, UNIT), :]
    own_row = lax.broadcasted_iota(jnp.int32, (UNIT, K), 0)
    own_slot = lax.broadcasted_iota(jnp.int32, (UNIT, K), 1)
    own_place = (own_slot // 2) * 8 + lax.rem(own_slot, 2) + 2 * own_row
    far_slot = lax.broadcasted_iota(jnp.int32, (K, K), 0)
    far_place = (far_slot // 2) * 8 + lax.rem(far_slot, 2)
    wide = lax.broadcasted_iota(jnp.int32, (UNIT, B), 1)
    drawn[...] = jnp.zeros((TABLE, B), jnp.int32)
    for rank in range(5):
        step = (0, -1, 1, 2, -2)[rank]
        far_unit = lax.rem(unit + step * (1 - 2 * core) + 128, 128)
        for cc in range(UNIT):
            far = jnp.transpose(jnp.broadcast_to(rows_held[pl.ds(UNIT * far_unit + cc, 1), :], (K, K)))
            rights = []
            for i in range(UNIT):
                fits = far == jnp.broadcast_to(columns[i : i + 1], (K, K))
                found = jnp.sum(jnp.where(fits, far_place + 2 * cc + 1, 0), axis=0, keepdims=True)
                rights.append(jnp.where(found == 0, HELD, jnp.minimum(found - 1, HELD)))
            right = jnp.concatenate(rights, axis=0)
            found = jnp.sum(
                jnp.where(columns == UNIT * far_unit + cc, own_place + 1, 0), axis=1, keepdims=True
            )
            left = jnp.where(found == 0, HELD, jnp.minimum(found - 1, HELD))
            at = (rank * UNIT + cc) * UNIT
            drawn[at : at + UNIT, :] = jnp.where(wide < K, jnp.tile(right, (1, B // K)), left)
    for d in range(3):
        corner = corners_held[d, pl.ds(UNIT * unit, UNIT), :]
        if d == 0:
            corner = lax.rem(corner - 16 * owner + 8 + 256, 256)
        at = CORNERS + d * UNIT
        drawn[at : at + UNIT, 0:K] = corner
    fetch = pltpu.make_async_copy(drawn, index, table_sem.at[2])
    fetch.start()
    fetch.wait()

    def part(ref, c):
        return ref.at[pl.ds(2 * UNIT * c, 2 * UNIT)]

    def forward(f, c):
        return pltpu.make_async_remote_copy(
            src_ref=part(held[f], c),
            dst_ref=part(held[2 + f], c),
            send_sem=fwd_send.at[f, c],
            recv_sem=fwd_recv.at[f, c],
            device_id=partner,
            device_id_type=MESH,
        )

    def wait_for(kind, c):
        slot = part(held[4 if kind == 2 else kind], c)
        pltpu.make_async_copy(slot, slot, recv_sem.at[kind, c]).wait()

    for f in range(2):

        @pl.loop(0, COLS)
        def _(c):
            wait_for(f, c)
            forward(f, c).start()

    def product(rank, i, pair):
        out = jnp.zeros((B, 2 * B), jnp.float32)
        for kk in range(0, UNIT, 2):
            lefts = [held0[index[(rank * UNIT + kk + e) * UNIT + i, K]] for e in range(2)]
            rights = []
            for e in range(2):
                at = (rank * UNIT + kk + e) * UNIT + i
                rights.append(
                    jnp.concatenate([held[rank][index[at, 2 * pair + f]] for f in range(2)], axis=1)
                )
            out += jnp.dot(
                jnp.concatenate(lefts, axis=1), jnp.concatenate(rights, axis=0), preferred_element_type=jnp.float32
            )
        return out

    for rank in range(4):
        if rank >= 2:

            @pl.loop(0, COLS)
            def _(c):
                forward(rank - 2, c).wait()

        @pl.loop(0, UNIT * K // 2)
        def _(at):
            value = product(rank, at // (K // 2), lax.rem(at, K // 2))
            sums[at] = value if rank == 0 else sums[at] + value

    @pl.loop(0, COLS)
    def _(c):
        wait_for(2, c)

    def goes_back(kind, c):
        src, dst, to_row = (
            (density.at[pl.ds(2 * UNIT * c, 2 * UNIT)], square.at[pl.ds(2 * UNIT * u_back, 2 * UNIT)], owner),
            (mid.at[pl.ds(16 * c, 16)], own.at[u_back], owner),
            (low.at[pl.ds(8 * c, 8)], above.at[u_back], down),
            (high.at[pl.ds(8 * c, 8)], below.at[u_back], up),
        )[kind]
        away = pltpu.make_async_remote_copy(
            src_ref=src,
            dst_ref=dst,
            send_sem=back_send.at[kind, c],
            recv_sem=back_recv.at[kind, u_back],
            device_id=(to_row, c),
            device_id_type=MESH,
        )
        return src, dst, back_recv.at[kind, u_back], away, jnp.logical_and(to_row == row, c == col)

    def start_back(kind, c):
        src, dst, sem, away, is_here = goes_back(kind, c)

        @pl.when(is_here)
        def _():
            pltpu.make_async_copy(src, dst, sem).start()

        @pl.when(jnp.logical_not(is_here))
        def _():
            away.start()

    @pl.loop(0, COLS)
    def _(w):
        pair = lax.rem(w + col, COLS)

        @pl.loop(0, UNIT)
        def _(i):
            value = (sums[i * (K // 2) + pair] + product(4, i, pair)).astype(jnp.bfloat16)
            for e in range(2):
                density[2 * UNIT * pair + 2 * i + e] = value[:, e * B : (e + 1) * B]

        start_back(0, pair)

    @pl.loop(0, UNIT)
    def _(i):
        @pl.loop(0, K // 2)
        def _(pair):
            for e in range(2):
                tile = 2 * pair + e
                placed = pltpu.roll(planes[...], index[CORNERS + i, tile], 0).astype(jnp.bfloat16)
                half = jnp.dot(placed, density[2 * UNIT * pair + 2 * i + e], preferred_element_type=jnp.float32)
                halves[pl.ds(pl.multiple_of(tile * 32, 32), 32), :] = half.astype(jnp.bfloat16)

        @pl.loop(0, K // 4)
        def _(four):
            rows = pl.ds(pl.multiple_of(four * 128, 128), 128)
            shifts = [index[CORNERS + 2 * UNIT + i, 4 * four + e] for e in range(4)]
            for b in range(0, 16, 2):
                values = jnp.dot(
                    halves[rows, :], cells[:, b * 128 : (b + 2) * 128], preferred_element_type=jnp.float32
                )
                for e in range(4):
                    for f in range(2):
                        piece = values[e * 32 : (e + 1) * 32, f * 128 : (f + 1) * 128]
                        tiles[(i * K + 4 * four + e) * SPAN + PAD + b + f] = pltpu.roll(piece, shifts[e], 1)

    @pl.loop(0, COLS)
    def _(w):
        c = lax.rem(w + col, COLS)

        @pl.loop(0, 2)
        def _(h):
            eight = 2 * c + h

            def add_tile(tile, values):
                off = 8 * eight - index[CORNERS + UNIT + tile // K, lax.rem(tile, K)]
                inside = jnp.logical_and(off > -PAD, off < 16)
                start = tile * SPAN + jnp.where(inside, off + PAD, 0)
                return tuple(value + tiles[start + y] for y, value in enumerate(values))

            values = lax.fori_loop(
                0, UNIT * K, add_tile, tuple(jnp.zeros((32, B), jnp.float32) for _ in range(8)), unroll=2
            )
            for y in range(8):
                mid[8 * eight + y] = values[y][8:24].astype(jnp.bfloat16)
            for y in range(4):
                first, second = values[2 * y], values[2 * y + 1]
                low[4 * eight + y] = jnp.concatenate([first[0:8], second[0:8]], axis=0).astype(jnp.bfloat16)
                high[4 * eight + y] = jnp.concatenate([first[24:32], second[24:32]], axis=0).astype(jnp.bfloat16)

        for kind in (1, 2, 3):
            start_back(kind, c)

    @pl.loop(0, 8)
    def _(v):
        refs = (square.at[pl.ds(2 * UNIT * v, 2 * UNIT)], own.at[v], above.at[v], below.at[v])
        for kind, ref in enumerate(refs):
            pltpu.make_async_copy(ref, ref, back_recv.at[kind, v]).wait()

    def added(ref, at):
        value = ref[0, at].astype(jnp.float32)
        for v in range(1, 8):
            value += ref[v, at].astype(jnp.float32)
        return value

    @pl.loop(0, 8)
    def _(yy):
        under, over = added(below, yy), added(above, yy)
        for e in range(2):
            rims = jnp.concatenate([under[8 * e : 8 * e + 8], over[8 * e : 8 * e + 8]], axis=0)
            at = pl.multiple_of((2 * yy + e) * 16, 16)
            total[pl.ds(at, 16), :] = added(own, 2 * yy + e) + rims

    for x in range(16):
        grid[x] = total[pl.ds(x, 16, stride=16), :]

    @pl.loop(0, 4)
    def _(v):
        for item in plan:
            away, is_here = sends(v, *item)[3:]

            @pl.when(jnp.logical_not(is_here))
            def _():
                away.wait_send()

    @pl.loop(0, COLS)
    def _(c):
        for kind in range(4):
            away, is_here = goes_back(kind, c)[3:]

            @pl.when(jnp.logical_not(is_here))
            def _():
                away.wait_send()


def fused(pattern, anchors, blocks, basis_x, basis_yz):
    return pl.pallas_call(
        kernel,
        out_shape=[
            jax.ShapeDtypeStruct((64, B, B), jnp.bfloat16),
            jax.ShapeDtypeStruct((16, 16, 128), jnp.float32),
        ],
        in_specs=[ANY, ANY, ANY, VMEM, VMEM],
        out_specs=[ANY, VMEM],
        scratch_shapes=[pltpu.VMEM((HELD + 1, B, B), jnp.bfloat16)] * 5
        + [
            pltpu.VMEM((UNIT * K // 2, B, 2 * B), jnp.float32),
            pltpu.VMEM((HELD, B, B), jnp.bfloat16),
            pltpu.VMEM((K * 32, B), jnp.bfloat16),
            pltpu.VMEM((UNIT * K * SPAN, 32, 128), jnp.float32),
            pltpu.VMEM((128, 16, 128), jnp.bfloat16),
            pltpu.VMEM((64, 16, 128), jnp.bfloat16),
            pltpu.VMEM((64, 16, 128), jnp.bfloat16),
            pltpu.VMEM((8, 16, 16, 128), jnp.bfloat16),
            pltpu.VMEM((8, 8, 16, 128), jnp.bfloat16),
            pltpu.VMEM((8, 8, 16, 128), jnp.bfloat16),
            pltpu.VMEM((256, 128), jnp.float32),
            pltpu.VMEM((NBR, K), jnp.int32),
            pltpu.VMEM((3, NBR, K), jnp.int32),
            pltpu.VMEM((32, B), jnp.float32),
            pltpu.VMEM((B, 16 * B), jnp.bfloat16),
            pltpu.VMEM((TABLE, B), jnp.int32),
            pltpu.SMEM((TABLE, B), jnp.int32),
            pltpu.SemaphoreType.DMA((8, 3)),
            pltpu.SemaphoreType.DMA((3, COLS)),
            pltpu.SemaphoreType.DMA((2, COLS)),
            pltpu.SemaphoreType.DMA((2, COLS)),
            pltpu.SemaphoreType.DMA((4, COLS)),
            pltpu.SemaphoreType.DMA((4, 8)),
            pltpu.SemaphoreType.DMA((3,)),
        ],
        compiler_params=pltpu.CompilerParams(collective_id=0, has_side_effects=True, vmem_limit_bytes=60 << 20),
        name="square_and_tiles",
    )(pattern, anchors, blocks, basis_x, basis_yz)


def per_device(blocks, pattern, anchors, basis_x, basis_yz):
    square, grid = fused(pattern, anchors, blocks.reshape(64, B, B), basis_x, basis_yz)
    return square.reshape(32, 2, B, B).astype(jnp.float32), grid


def solution(mesh):
    placed = (P("row", "col", None, None), P(), P(), P(), P())
    return jax.shard_map(
        per_device,
        mesh=mesh,
        in_specs=placed,
        out_specs=(P("row", "col", None, None), P("row", "col", None)),
        check_vma=False,
    )
```

```python
import jax
import jax.numpy as jnp
from jax import lax
from jax.experimental import pallas as pl
from jax.experimental.pallas import tpu as pltpu
from jax.sharding import PartitionSpec as P

MESH = pl.DeviceIdType.MESH
B = 128
K = 16
H = 8
UNIT = 4
ROWS = 16
COLS = 8
SHARES = 64
NBR = 512
HELD = UNIT * K
CORNERS = 5 * UNIT * UNIT
TABLE = 96
PAD = 8
SPAN = 32
ANY = pl.BlockSpec(memory_space=pl.ANY)
VMEM = pl.BlockSpec(memory_space=pltpu.VMEM)
SMEM = pl.BlockSpec(memory_space=pltpu.SMEM)


def col_of_place(place):
    return place


def place_of_col(col):
    return col


def device_of(share, core):
    share = lax.rem(share + SHARES, SHARES)
    return 2 * (share // 8) + core, col_of_place(lax.rem(share, 8))


def signal(sem, row, col):
    pl.semaphore_signal(sem, inc=1, device_id=(row, col), device_id_type=MESH)


def kernel(
    pattern, anchors, blocks, basis_x, basis_yz,
    square, grid,
    held0, held1, held2, held3, held4, sums, density, halves, tiles, mid, low, high, own, below, above, total, other_mid, other_low, other_high,
    rows_held, corners_held, planes, cells, drawn, index,
    send_sem, recv_sem, fwd_send, fwd_recv, back_send, back_recv, share_send, share_recv, table_sem,
):
    row = lax.axis_index("row")
    col = lax.axis_index("col")
    core = lax.rem(row, 2)
    share = (row // 2) * 8 + place_of_col(col)
    partner = (row + 1 - 2 * core, col)
    unit = 2 * share + core
    owner = unit // 8
    u_back = lax.rem(unit, 8)
    up = lax.rem(owner + 1, ROWS)
    down = lax.rem(owner + ROWS - 1, ROWS)
    held = (held0, held1, held2, held3, held4)

    barrier = pltpu.get_barrier_semaphore()
    first_unit = 2 * share - 2 + 3 * core + 128
    row_a = lax.rem(first_unit // 8, ROWS)
    row_b = lax.rem((first_unit + 2) // 8, ROWS)

    @pl.loop(0, COLS)
    def _(c):
        @pl.when(jnp.logical_or(row_a != row, c != col))
        def _():
            signal(barrier, row_a, c)

        @pl.when(jnp.logical_and(row_b != row_a, jnp.logical_or(row_b != row, c != col)))
        def _():
            signal(barrier, row_b, c)

    @pl.loop(0, 12)
    def _(v):
        from_share = 4 * (row - 1) + v

        @pl.loop(0, 2)
        def _(e):
            from_row, from_col = device_of(from_share + SHARES, e)
            sends_here = jnp.logical_or(v // 4 == 1, e == lax.rem(col, 2))

            @pl.when(jnp.logical_and(sends_here, jnp.logical_or(from_row != row, from_col != col)))
            def _():
                signal(barrier, from_row, from_col)

    signal(barrier, *partner)
    place = lax.rem(share, 8)
    is_own = jnp.where(core == 0, place <= 4, place >= 3).astype(jnp.int32)
    beside = jnp.logical_and(jnp.logical_or(up == row, down == row), lax.rem(col, 2) == core)
    is_goal = jnp.logical_or(owner == row, beside).astype(jnp.int32)
    pl.semaphore_wait(barrier, 27 - is_own - is_goal)

    plan = ((0, 1, 0, 1), (0, 0, 0, 0), (1, 0, -1, 1), (1, 1, 1, 0), (2, 0, 1, 0), (2, 1, -1, 1))

    def sends(v, kind, parity, step, goal_core):
        u = 2 * v + parity
        goal_row, goal_col = device_of(4 * row + v + step, goal_core)
        src = blocks.at[pl.ds(2 * UNIT * u, 2 * UNIT)]
        dst = held[4 if kind == 2 else kind].at[pl.ds(2 * UNIT * col, 2 * UNIT)]
        away = pltpu.make_async_remote_copy(
            src_ref=src,
            dst_ref=dst,
            send_sem=send_sem.at[u, kind],
            recv_sem=recv_sem.at[kind, col],
            device_id=(goal_row, goal_col),
            device_id_type=MESH,
        )
        is_here = jnp.logical_and(goal_row == row, goal_col == col)
        return src, dst, recv_sem.at[kind, col], away, is_here

    def start_kind(kind):
        @pl.loop(0, 4)
        def _(w):
            v = lax.rem(w + col // 2, 4)
            for item in plan[2 * kind : 2 * kind + 2]:
                src, dst, sem, away, is_here = sends(v, *item)

                @pl.when(is_here)
                def _():
                    pltpu.make_async_copy(src, dst, sem).start()

                @pl.when(jnp.logical_not(is_here))
                def _():
                    away.start()

    start_kind(0)
    start_kind(1)

    loads = (
        pltpu.make_async_copy(pattern, rows_held, table_sem.at[0]),
        pltpu.make_async_copy(anchors, corners_held, table_sem.at[1]),
    )
    for load in loads:
        load.start()
    for ref in held:
        ref[HELD] = jnp.zeros((B, B), jnp.bfloat16)

    planes[...] = jnp.concatenate([basis_x[...].astype(jnp.float32), jnp.zeros((16, B), jnp.float32)], axis=0)
    lane = lax.broadcasted_iota(jnp.int32, (B, B), 1)
    for b in range(16):
        half = basis_yz[:, (b // 8) * B : (b // 8 + 1) * B].astype(jnp.float32)
        turned = pltpu.roll(half, (B - 16 * (b % 8)) % B, 1)
        cells[:, b * B : (b + 1) * B] = jnp.where(lane < 16, turned, 0.0).astype(jnp.bfloat16)

    @pl.loop(0, UNIT * K)
    def _(tile):
        for e in range(PAD):
            tiles[tile * SPAN + e] = jnp.zeros((32, B), jnp.bfloat16)
            tiles[tile * SPAN + PAD + 16 + e] = jnp.zeros((32, B), jnp.bfloat16)

    for load in loads:
        load.wait()
    window = pltpu.roll(rows_held[...], lax.rem(2 * NBR + H - UNIT * unit, NBR), 1)[:, :B]
    columns = jnp.transpose(window)[H : H + UNIT]
    own_row = lax.broadcasted_iota(jnp.int32, (UNIT, K), 0)
    own_slot = lax.broadcasted_iota(jnp.int32, (UNIT, K), 1)
    own_place = (own_slot // 2) * 8 + lax.rem(own_slot, 2) + 2 * own_row
    far_slot = lax.broadcasted_iota(jnp.int32, (K, K), 0)
    far_place = (far_slot // 2) * 8 + lax.rem(far_slot, 2)
    wide = lax.broadcasted_iota(jnp.int32, (UNIT, B), 1)
    drawn[...] = jnp.zeros((TABLE, B), jnp.int32)
    for rank in range(5):
        step = (0, -1, 1, 2, -2)[rank]
        far_unit = lax.rem(unit + step * (1 - 2 * core) + 128, 128)
        for cc in range(UNIT):
            lanes = [UNIT * (2 + sign * step) + cc for sign in (1, -1)]
            far = jnp.where(core == 0, *[window[:, lane : lane + 1] for lane in lanes])
            far = jnp.broadcast_to(far, (K, K))
            rights = []
            for i in range(UNIT):
                fits = far == jnp.broadcast_to(columns[i : i + 1], (K, K))
                found = jnp.sum(jnp.where(fits, far_place + 2 * cc + 1, 0), axis=0, keepdims=True)
                rights.append(jnp.where(found == 0, HELD, jnp.minimum(found - 1, HELD)))
            right = jnp.concatenate(rights, axis=0)
            found = jnp.sum(
                jnp.where(columns == UNIT * far_unit + cc, own_place + 1, 0), axis=1, keepdims=True
            )
            left = jnp.where(found == 0, HELD, jnp.minimum(found - 1, HELD))
            at = (rank * UNIT + cc) * UNIT
            drawn[at : at + UNIT, :] = jnp.where(wide < K, jnp.tile(right, (1, B // K)), left)
    for d in range(3):
        corner = pltpu.roll(corners_held[d], lax.rem(NBR - UNIT * unit, NBR), 1)[:, :B]
        corner = jnp.transpose(corner)[:UNIT]
        if d == 0:
            corner = lax.rem(corner - 16 * owner + 8 + 256, 256)
        at = CORNERS + d * UNIT
        drawn[at : at + UNIT, 0:K] = corner
    fetch = pltpu.make_async_copy(drawn, index, table_sem.at[2])
    fetch.start()
    fetch.wait()

    def part(ref, c):
        return ref.at[pl.ds(2 * UNIT * c, 2 * UNIT)]

    def forward(f, c):
        return pltpu.make_async_remote_copy(
            src_ref=part(held[f], c),
            dst_ref=part(held[2 + f], c),
            send_sem=fwd_send.at[f, c],
            recv_sem=fwd_recv.at[f, c],
            device_id=partner,
            device_id_type=MESH,
        )

    def wait_for(kind, c):
        slot = part(held[4 if kind == 2 else kind], c)
        pltpu.make_async_copy(slot, slot, recv_sem.at[kind, c]).wait()

    for f in range(2):

        @pl.loop(0, COLS)
        def _(c):
            wait_for(f, c)
            forward(f, c).start()

        if f == 0:
            start_kind(2)

    def product(rank, i, pair):
        out = jnp.zeros((B, 2 * B), jnp.float32)
        for kk in range(0, UNIT, 2):
            lefts = [held0[index[(rank * UNIT + kk + e) * UNIT + i, K]] for e in range(2)]
            rights = []
            for e in range(2):
                at = (rank * UNIT + kk + e) * UNIT + i
                rights.append(
                    jnp.concatenate([held[rank][index[at, 2 * pair + f]] for f in range(2)], axis=1)
                )
            out += jnp.dot(
                jnp.concatenate(lefts, axis=1), jnp.concatenate(rights, axis=0), preferred_element_type=jnp.float32
            )
        return out

    for rank in range(4):
        if rank >= 2:

            @pl.loop(0, COLS)
            def _(c):
                forward(rank - 2, c).wait()

        @pl.loop(0, UNIT * K // 2, unroll=4)
        def _(at):
            value = product(rank, at // (K // 2), lax.rem(at, K // 2))
            sums[at] = value if rank == 0 else sums[at] + value

    @pl.loop(0, COLS)
    def _(c):
        wait_for(2, c)

    def goes_back(kind, c):
        src, dst, to_row = (
            (density.at[pl.ds(2 * UNIT * c, 2 * UNIT)], square.at[pl.ds(2 * UNIT * u_back, 2 * UNIT)], owner),
            (mid.at[pl.ds(16 * c, 16)], own.at[u_back // 2], owner),
            (low.at[pl.ds(8 * c, 8)], above.at[u_back // 2], down),
            (high.at[pl.ds(8 * c, 8)], below.at[u_back // 2], up),
        )[kind]
        slot = u_back if kind == 0 else u_back // 2
        away = pltpu.make_async_remote_copy(
            src_ref=src,
            dst_ref=dst,
            send_sem=back_send.at[kind, c],
            recv_sem=back_recv.at[kind, slot],
            device_id=(to_row, c),
            device_id_type=MESH,
        )
        return src, dst, back_recv.at[kind, slot], away, jnp.logical_and(to_row == row, c == col)

    def start_back(kind, c):
        src, dst, sem, away, is_here = goes_back(kind, c)

        @pl.when(is_here)
        def _():
            pltpu.make_async_copy(src, dst, sem).start()

        @pl.when(jnp.logical_not(is_here))
        def _():
            away.start()

    @pl.loop(0, COLS)
    def _(w):
        pair = lax.rem(w + col, COLS)

        @pl.loop(0, UNIT, unroll=4)
        def _(i):
            value = (sums[i * (K // 2) + pair] + product(4, i, pair)).astype(jnp.bfloat16)
            for e in range(2):
                density[2 * UNIT * pair + 2 * i + e] = value[:, e * B : (e + 1) * B]

        start_back(0, pair)

    @pl.loop(0, UNIT)
    def _(i):
        for pair in range(K // 2):
            for e in range(2):
                tile = 2 * pair + e
                placed = pltpu.roll(planes[...], index[CORNERS + i, tile], 0).astype(jnp.bfloat16)
                half = jnp.dot(placed, density[2 * UNIT * pair + 2 * i + e], preferred_element_type=jnp.float32)
                halves[pl.ds(pl.multiple_of(tile * 32, 32), 32), :] = half.astype(jnp.bfloat16)

        @pl.loop(0, K // 4)
        def _(four):
            rows = pl.ds(pl.multiple_of(four * 128, 128), 128)
            shifts = [index[CORNERS + 2 * UNIT + i, 4 * four + e] for e in range(4)]
            for b in range(0, 16, 2):
                values = jnp.dot(
                    halves[rows, :], cells[:, b * 128 : (b + 2) * 128], preferred_element_type=jnp.float32
                )
                for e in range(4):
                    for f in range(2):
                        piece = values[e * 32 : (e + 1) * 32, f * 128 : (f + 1) * 128]
                        tiles[(i * K + 4 * four + e) * SPAN + PAD + b + f] = pltpu.roll(piece, shifts[e], 1).astype(
                            jnp.bfloat16
                        )

    def partial(eight):
        def add_tile(tile, values):
            off = 8 * eight - index[CORNERS + UNIT + tile // K, lax.rem(tile, K)]
            inside = jnp.logical_and(off > -PAD, off < 16)
            start = tile * SPAN + jnp.where(inside, off + PAD, 0)
            return tuple(value + tiles[start + y].astype(jnp.float32) for y, value in enumerate(values))

        zeros = tuple(jnp.zeros((32, B), jnp.float32) for _ in range(8))
        values = lax.fori_loop(0, UNIT * K, add_tile, zeros, unroll=8)
        pairs = [values[2 * y : 2 * y + 2] for y in range(4)]
        mids = [value[8:24] for value in values]
        lows = [jnp.concatenate([first[0:8], second[0:8]], axis=0) for first, second in pairs]
        highs = [jnp.concatenate([first[24:32], second[24:32]], axis=0) for first, second in pairs]
        return mids, lows, highs

    def share_parts(kind, c):
        ref, other = ((mid, other_mid), (low, other_low), (high, other_high))[kind]
        size = 16 if kind == 0 else 8
        return pltpu.make_async_remote_copy(
            src_ref=ref.at[pl.ds(size * c, size)],
            dst_ref=other.at[c // 2],
            send_sem=share_send.at[kind, c // 2],
            recv_sem=share_recv.at[kind, c // 2],
            device_id=partner,
            device_id_type=MESH,
        )

    @pl.loop(0, COLS // 2)
    def _(w):
        c = 2 * lax.rem(w + col // 2, COLS // 2) + 1 - core

        @pl.loop(0, 2)
        def _(h):
            for ref, values in zip((mid, low, high), partial(2 * c + h)):
                for y, value in enumerate(values):
                    ref[(2 * c + h) * len(values) + y] = value.astype(jnp.bfloat16)

        for kind in range(3):
            share_parts(kind, c).start()

    @pl.loop(0, COLS // 2)
    def _(w):
        c = 2 * lax.rem(w + col // 2, COLS // 2) + core
        for kind in range(3):
            share_parts(kind, c).wait_recv()

        @pl.loop(0, 2)
        def _(h):
            others = (other_mid, other_low, other_high)
            for ref, other, values in zip((mid, low, high), others, partial(2 * c + h)):
                for y, value in enumerate(values):
                    value += other[c // 2, h * len(values) + y].astype(jnp.float32)
                    ref[(2 * c + h) * len(values) + y] = value.astype(jnp.bfloat16)

        for kind in (1, 2, 3):
            start_back(kind, c)

    @pl.loop(0, 8)
    def _(v):
        ref = square.at[pl.ds(2 * UNIT * v, 2 * UNIT)]
        pltpu.make_async_copy(ref, ref, back_recv.at[0, v]).wait()

    @pl.loop(0, 4)
    def _(v):
        for kind, ref in enumerate((own.at[v], above.at[v], below.at[v])):
            pltpu.make_async_copy(ref, ref, back_recv.at[kind + 1, v]).wait()

    def added(ref, at):
        value = ref[0, at].astype(jnp.float32)
        for v in range(1, 4):
            value += ref[v, at].astype(jnp.float32)
        return value

    @pl.loop(0, 8)
    def _(yy):
        under, over = added(below, yy), added(above, yy)
        for e in range(2):
            rims = jnp.concatenate([under[8 * e : 8 * e + 8], over[8 * e : 8 * e + 8]], axis=0)
            at = pl.multiple_of((2 * yy + e) * 16, 16)
            total[pl.ds(at, 16), :] = added(own, 2 * yy + e) + rims

    for x in range(16):
        grid[x] = total[pl.ds(x, 16, stride=16), :]

    @pl.loop(0, 4)
    def _(v):
        for item in plan:
            away, is_here = sends(v, *item)[3:]

            @pl.when(jnp.logical_not(is_here))
            def _():
                away.wait_send()

    def end_back(kind, c):
        away, is_here = goes_back(kind, c)[3:]

        @pl.when(jnp.logical_not(is_here))
        def _():
            away.wait_send()

    @pl.loop(0, COLS)
    def _(c):
        end_back(0, c)

    @pl.loop(0, COLS // 2)
    def _(w):
        for kind in range(3):
            share_parts(kind, 2 * w + 1 - core).wait_send()
            end_back(kind + 1, 2 * w + core)


def fused(pattern, anchors, blocks, basis_x, basis_yz):
    return pl.pallas_call(
        kernel,
        out_shape=[
            jax.ShapeDtypeStruct((64, B, B), jnp.bfloat16),
            jax.ShapeDtypeStruct((16, 16, 128), jnp.float32),
        ],
        in_specs=[ANY, ANY, ANY, VMEM, VMEM],
        out_specs=[ANY, VMEM],
        scratch_shapes=[pltpu.VMEM((HELD + 1, B, B), jnp.bfloat16)] * 5
        + [
            pltpu.VMEM((UNIT * K // 2, B, 2 * B), jnp.float32),
            pltpu.VMEM((HELD, B, B), jnp.bfloat16),
            pltpu.VMEM((K * 32, B), jnp.bfloat16),
            pltpu.VMEM((UNIT * K * SPAN, 32, 128), jnp.bfloat16),
            pltpu.VMEM((128, 16, 128), jnp.bfloat16),
            pltpu.VMEM((64, 16, 128), jnp.bfloat16),
            pltpu.VMEM((64, 16, 128), jnp.bfloat16),
            pltpu.VMEM((4, 16, 16, 128), jnp.bfloat16),
            pltpu.VMEM((4, 8, 16, 128), jnp.bfloat16),
            pltpu.VMEM((4, 8, 16, 128), jnp.bfloat16),
            pltpu.VMEM((256, 128), jnp.float32),
            pltpu.VMEM((4, 16, 16, 128), jnp.bfloat16),
            pltpu.VMEM((4, 8, 16, 128), jnp.bfloat16),
            pltpu.VMEM((4, 8, 16, 128), jnp.bfloat16),
            pltpu.VMEM((K, NBR), jnp.int32),
            pltpu.VMEM((3, K, NBR), jnp.int32),
            pltpu.VMEM((32, B), jnp.float32),
            pltpu.VMEM((B, 16 * B), jnp.bfloat16),
            pltpu.VMEM((TABLE, B), jnp.int32),
            pltpu.SMEM((TABLE, B), jnp.int32),
            pltpu.SemaphoreType.DMA((8, 3)),
            pltpu.SemaphoreType.DMA((3, COLS)),
            pltpu.SemaphoreType.DMA((2, COLS)),
            pltpu.SemaphoreType.DMA((2, COLS)),
            pltpu.SemaphoreType.DMA((4, COLS)),
            pltpu.SemaphoreType.DMA((4, 8)),
            pltpu.SemaphoreType.DMA((3, 4)),
            pltpu.SemaphoreType.DMA((3, 4)),
            pltpu.SemaphoreType.DMA((3,)),
        ],
        compiler_params=pltpu.CompilerParams(collective_id=0, has_side_effects=True, vmem_limit_bytes=60 << 20),
        name="square_and_tiles",
    )(pattern, anchors, blocks, basis_x, basis_yz)


def per_device(blocks, pattern, anchors, basis_x, basis_yz):
    square, grid = fused(pattern.T, jnp.transpose(anchors, (0, 2, 1)), blocks.reshape(64, B, B), basis_x, basis_yz)
    return square.reshape(32, 2, B, B).astype(jnp.float32), grid


def solution(mesh):
    placed = (P("row", "col", None, None), P(), P(), P(), P())
    return jax.shard_map(
        per_device,
        mesh=mesh,
        in_specs=placed,
        out_specs=(P("row", "col", None, None), P("row", "col", None)),
        check_vma=False,
    )
```

```python
import jax
import jax.numpy as jnp
from jax import lax
from jax.experimental import pallas as pl
from jax.experimental.pallas import tpu as pltpu
from jax.sharding import PartitionSpec as P

MESH = pl.DeviceIdType.MESH
B = 128
K = 16
H = 8
UNIT = 4
ROWS = 16
COLS = 8
SHARES = 64
NBR = 512
HELD = UNIT * K
CORNERS = 5 * UNIT * UNIT
TABLE = 96
PAD = 8
SPAN = 32
ANY = pl.BlockSpec(memory_space=pl.ANY)
VMEM = pl.BlockSpec(memory_space=pltpu.VMEM)
SMEM = pl.BlockSpec(memory_space=pltpu.SMEM)


def col_of_place(place):
    return place


def place_of_col(col):
    return col


def device_of(share, core):
    share = lax.rem(share + SHARES, SHARES)
    return 2 * (share // 8) + core, col_of_place(lax.rem(share, 8))


def signal(sem, row, col):
    pl.semaphore_signal(sem, inc=1, device_id=(row, col), device_id_type=MESH)


def kernel(
    pattern, anchors, blocks, basis_x, basis_yz,
    square, grid,
    held0, held1, held2, held3, held4, sums, density, halves, tiles, mid, low, high, own, below, above, total, other_mid, other_low, other_high,
    rows_held, corners_held, planes, cells, drawn, index,
    send_sem, recv_sem, fwd_send, fwd_recv, back_send, back_recv, share_send, share_recv, table_sem,
):
    row = lax.axis_index("row")
    col = lax.axis_index("col")
    core = lax.rem(row, 2)
    share = (row // 2) * 8 + place_of_col(col)
    partner = (row + 1 - 2 * core, col)
    unit = 2 * share + core
    owner = unit // 8
    u_back = lax.rem(unit, 8)
    up = lax.rem(owner + 1, ROWS)
    down = lax.rem(owner + ROWS - 1, ROWS)
    held = (held0, held1, held2, held3, held4)

    barrier = pltpu.get_barrier_semaphore()
    first_unit = 2 * share - 2 + 3 * core + 128
    row_a = lax.rem(first_unit // 8, ROWS)
    row_b = lax.rem((first_unit + 2) // 8, ROWS)

    @pl.loop(0, COLS)
    def _(c):
        @pl.when(jnp.logical_or(row_a != row, c != col))
        def _():
            signal(barrier, row_a, c)

        @pl.when(jnp.logical_and(row_b != row_a, jnp.logical_or(row_b != row, c != col)))
        def _():
            signal(barrier, row_b, c)

    @pl.loop(0, 12)
    def _(v):
        from_share = 4 * (row - 1) + v

        @pl.loop(0, 2)
        def _(e):
            from_row, from_col = device_of(from_share + SHARES, e)
            sends_here = jnp.logical_or(v // 4 == 1, e == lax.rem(col, 2))

            @pl.when(jnp.logical_and(sends_here, jnp.logical_or(from_row != row, from_col != col)))
            def _():
                signal(barrier, from_row, from_col)

    signal(barrier, *partner)
    place = lax.rem(share, 8)
    is_own = jnp.where(core == 0, place <= 4, place >= 3).astype(jnp.int32)
    beside = jnp.logical_and(jnp.logical_or(up == row, down == row), lax.rem(col, 2) == core)
    is_goal = jnp.logical_or(owner == row, beside).astype(jnp.int32)
    pl.semaphore_wait(barrier, 27 - is_own - is_goal)

    plan = ((0, 1, 0, 1), (0, 0, 0, 0), (1, 0, -1, 1), (1, 1, 1, 0), (2, 0, 1, 0), (2, 1, -1, 1))

    def sends(v, kind, parity, step, goal_core):
        u = 2 * v + parity
        goal_row, goal_col = device_of(4 * row + v + step, goal_core)
        src = blocks.at[pl.ds(2 * UNIT * u, 2 * UNIT)]
        dst = held[4 if kind == 2 else kind].at[pl.ds(2 * UNIT * col, 2 * UNIT)]
        away = pltpu.make_async_remote_copy(
            src_ref=src,
            dst_ref=dst,
            send_sem=send_sem.at[u, kind],
            recv_sem=recv_sem.at[kind, col],
            device_id=(goal_row, goal_col),
            device_id_type=MESH,
        )
        is_here = jnp.logical_and(goal_row == row, goal_col == col)
        return src, dst, recv_sem.at[kind, col], away, is_here

    def start_kind(kind):
        @pl.loop(0, 4)
        def _(w):
            v = lax.rem(w + col // 2, 4)
            for item in plan[2 * kind : 2 * kind + 2]:
                src, dst, sem, away, is_here = sends(v, *item)

                @pl.when(is_here)
                def _():
                    pltpu.make_async_copy(src, dst, sem).start()

                @pl.when(jnp.logical_not(is_here))
                def _():
                    away.start()

    start_kind(0)
    start_kind(1)

    loads = (
        pltpu.make_async_copy(pattern, rows_held, table_sem.at[0]),
        pltpu.make_async_copy(anchors, corners_held, table_sem.at[1]),
    )
    for load in loads:
        load.start()
    for ref in held:
        ref[HELD] = jnp.zeros((B, B), jnp.bfloat16)

    planes[...] = jnp.concatenate([basis_x[...].astype(jnp.float32), jnp.zeros((16, B), jnp.float32)], axis=0)
    lane = lax.broadcasted_iota(jnp.int32, (B, B), 1)
    for b in range(16):
        half = basis_yz[:, (b // 8) * B : (b // 8 + 1) * B].astype(jnp.float32)
        turned = pltpu.roll(half, (B - 16 * (b % 8)) % B, 1)
        cells[:, b * B : (b + 1) * B] = jnp.where(lane < 16, turned, 0.0).astype(jnp.bfloat16)

    @pl.loop(0, UNIT * K)
    def _(tile):
        for e in range(PAD):
            tiles[tile * SPAN + e] = jnp.zeros((32, B), jnp.bfloat16)
            tiles[tile * SPAN + PAD + 16 + e] = jnp.zeros((32, B), jnp.bfloat16)

    for load in loads:
        load.wait()
    window = pltpu.roll(rows_held[...], lax.rem(2 * NBR + H - UNIT * unit, NBR), 1)[:, :B]
    columns = jnp.transpose(window)[H : H + UNIT]
    own_row = lax.broadcasted_iota(jnp.int32, (UNIT, K), 0)
    own_slot = lax.broadcasted_iota(jnp.int32, (UNIT, K), 1)
    own_place = (own_slot // 2) * 8 + lax.rem(own_slot, 2) + 2 * own_row
    far_slot = lax.broadcasted_iota(jnp.int32, (K, K), 0)
    far_place = (far_slot // 2) * 8 + lax.rem(far_slot, 2)
    wide = lax.broadcasted_iota(jnp.int32, (UNIT, B), 1)
    drawn[...] = jnp.zeros((TABLE, B), jnp.int32)
    for rank in range(5):
        step = (0, -1, 1, 2, -2)[rank]
        far_unit = lax.rem(unit + step * (1 - 2 * core) + 128, 128)
        for cc in range(UNIT):
            lanes = [UNIT * (2 + sign * step) + cc for sign in (1, -1)]
            far = jnp.where(core == 0, *[window[:, lane : lane + 1] for lane in lanes])
            far = jnp.broadcast_to(far, (K, K))
            rights = []
            for i in range(UNIT):
                fits = far == jnp.broadcast_to(columns[i : i + 1], (K, K))
                found = jnp.sum(jnp.where(fits, far_place + 2 * cc + 1, 0), axis=0, keepdims=True)
                rights.append(jnp.where(found == 0, HELD, jnp.minimum(found - 1, HELD)))
            right = jnp.concatenate(rights, axis=0)
            found = jnp.sum(
                jnp.where(columns == UNIT * far_unit + cc, own_place + 1, 0), axis=1, keepdims=True
            )
            left = jnp.where(found == 0, HELD, jnp.minimum(found - 1, HELD))
            at = (rank * UNIT + cc) * UNIT
            drawn[at : at + UNIT, :] = jnp.where(wide < K, jnp.tile(right, (1, B // K)), left)
    for d in range(3):
        corner = pltpu.roll(corners_held[d], lax.rem(NBR - UNIT * unit, NBR), 1)[:, :B]
        corner = jnp.transpose(corner)[:UNIT]
        if d == 0:
            corner = lax.rem(corner - 16 * owner + 8 + 256, 256)
        at = CORNERS + d * UNIT
        drawn[at : at + UNIT, 0:K] = corner
    fetch = pltpu.make_async_copy(drawn, index, table_sem.at[2])
    fetch.start()
    fetch.wait()

    def part(ref, c):
        return ref.at[pl.ds(2 * UNIT * c, 2 * UNIT)]

    def forward(f, c):
        return pltpu.make_async_remote_copy(
            src_ref=part(held[f], c),
            dst_ref=part(held[2 + f], c),
            send_sem=fwd_send.at[f, c],
            recv_sem=fwd_recv.at[f, c],
            device_id=partner,
            device_id_type=MESH,
        )

    def wait_for(kind, c):
        slot = part(held[4 if kind == 2 else kind], c)
        pltpu.make_async_copy(slot, slot, recv_sem.at[kind, c]).wait()

    for f in range(2):

        @pl.loop(0, COLS)
        def _(c):
            wait_for(f, c)
            forward(f, c).start()

        if f == 0:
            start_kind(2)

    def product(rank, i, pair, parts=(0, 2)):
        out = jnp.zeros((B, 2 * B), jnp.float32)
        for kk in parts:
            lefts = [held0[index[(rank * UNIT + kk + e) * UNIT + i, K]] for e in range(2)]
            rights = []
            for e in range(2):
                at = (rank * UNIT + kk + e) * UNIT + i
                rights.append(
                    jnp.concatenate([held[rank][index[at, 2 * pair + f]] for f in range(2)], axis=1)
                )
            out += jnp.dot(
                jnp.concatenate(lefts, axis=1), jnp.concatenate(rights, axis=0), preferred_element_type=jnp.float32
            )
        return out

    for rank in range(4):
        if rank >= 2:

            @pl.loop(0, COLS)
            def _(c):
                forward(rank - 2, c).wait()

        @pl.loop(0, UNIT * K // 2, unroll=4)
        def _(at):
            value = product(rank, at // (K // 2), lax.rem(at, K // 2))
            sums[at] = value if rank == 0 else sums[at] + value

    @pl.loop(0, COLS)
    def _(c):
        wait_for(2, c)

    def goes_back(kind, c):
        src, dst, to_row = (
            (density.at[pl.ds(2 * UNIT * c, 2 * UNIT)], square.at[pl.ds(2 * UNIT * u_back, 2 * UNIT)], owner),
            (mid.at[pl.ds(16 * c, 16)], own.at[u_back // 2], owner),
            (low.at[pl.ds(8 * c, 8)], above.at[u_back // 2], down),
            (high.at[pl.ds(8 * c, 8)], below.at[u_back // 2], up),
        )[kind]
        slot = u_back if kind == 0 else u_back // 2
        away = pltpu.make_async_remote_copy(
            src_ref=src,
            dst_ref=dst,
            send_sem=back_send.at[kind, c],
            recv_sem=back_recv.at[kind, slot],
            device_id=(to_row, c),
            device_id_type=MESH,
        )
        return src, dst, back_recv.at[kind, slot], away, jnp.logical_and(to_row == row, c == col)

    def start_back(kind, c):
        src, dst, sem, away, is_here = goes_back(kind, c)

        @pl.when(is_here)
        def _():
            pltpu.make_async_copy(src, dst, sem).start()

        @pl.when(jnp.logical_not(is_here))
        def _():
            away.start()

    @pl.loop(0, COLS)
    def _(w):
        pair = lax.rem(w + col + 1, COLS)

        near, far = 2 * (1 - core), 2 * core
        for j in range(UNIT):
            i = far + j if j < 2 else near + j - 2
            value = sums[i * (K // 2) + pair] + product(4, i, pair, (near, far) if j < 2 else (near,))
            value = value.astype(jnp.bfloat16)
            for e in range(2):
                density[2 * UNIT * pair + 2 * i + e] = value[:, e * B : (e + 1) * B]

        start_back(0, pair)

    @pl.loop(0, UNIT)
    def _(i):
        for pair in range(K // 2):
            for e in range(2):
                tile = 2 * pair + e
                placed = pltpu.roll(planes[...], index[CORNERS + i, tile], 0).astype(jnp.bfloat16)
                half = jnp.dot(placed, density[2 * UNIT * pair + 2 * i + e], preferred_element_type=jnp.float32)
                halves[pl.ds(pl.multiple_of(tile * 32, 32), 32), :] = half.astype(jnp.bfloat16)

        @pl.loop(0, K // 4)
        def _(four):
            rows = pl.ds(pl.multiple_of(four * 128, 128), 128)
            shifts = [index[CORNERS + 2 * UNIT + i, 4 * four + e] for e in range(4)]
            for b in range(0, 16, 2):
                values = jnp.dot(
                    halves[rows, :], cells[:, b * 128 : (b + 2) * 128], preferred_element_type=jnp.float32
                )
                for e in range(4):
                    for f in range(2):
                        piece = values[e * 32 : (e + 1) * 32, f * 128 : (f + 1) * 128]
                        tiles[(i * K + 4 * four + e) * SPAN + PAD + b + f] = pltpu.roll(piece, shifts[e], 1).astype(
                            jnp.bfloat16
                        )

    def partial(eight):
        def add_tile(tile, values):
            off = 8 * eight - index[CORNERS + UNIT + tile // K, lax.rem(tile, K)]
            inside = jnp.logical_and(off > -PAD, off < 16)
            start = tile * SPAN + jnp.where(inside, off + PAD, 0)
            return tuple(value + tiles[start + y].astype(jnp.float32) for y, value in enumerate(values))

        zeros = tuple(jnp.zeros((32, B), jnp.float32) for _ in range(8))
        values = lax.fori_loop(0, UNIT * K, add_tile, zeros, unroll=16)
        pairs = [values[2 * y : 2 * y + 2] for y in range(4)]
        mids = [value[8:24] for value in values]
        lows = [jnp.concatenate([first[0:8], second[0:8]], axis=0) for first, second in pairs]
        highs = [jnp.concatenate([first[24:32], second[24:32]], axis=0) for first, second in pairs]
        return mids, lows, highs

    def share_parts(kind, c):
        ref, other = ((mid, other_mid), (low, other_low), (high, other_high))[kind]
        size = 16 if kind == 0 else 8
        return pltpu.make_async_remote_copy(
            src_ref=ref.at[pl.ds(size * c, size)],
            dst_ref=other.at[c // 2],
            send_sem=share_send.at[kind, c // 2],
            recv_sem=share_recv.at[kind, c // 2],
            device_id=partner,
            device_id_type=MESH,
        )

    @pl.loop(0, COLS // 2)
    def _(w):
        c = 2 * lax.rem(w + col // 2, COLS // 2) + 1 - core

        @pl.loop(0, 2)
        def _(h):
            for ref, values in zip((mid, low, high), partial(2 * c + h)):
                for y, value in enumerate(values):
                    ref[(2 * c + h) * len(values) + y] = value.astype(jnp.bfloat16)

        for kind in range(3):
            share_parts(kind, c).start()

    @pl.loop(0, COLS // 2)
    def _(w):
        c = 2 * lax.rem(w + col // 2, COLS // 2) + core
        for kind in range(3):
            share_parts(kind, c).wait_recv()

        @pl.loop(0, 2)
        def _(h):
            others = (other_mid, other_low, other_high)
            for ref, other, values in zip((mid, low, high), others, partial(2 * c + h)):
                for y, value in enumerate(values):
                    value += other[c // 2, h * len(values) + y].astype(jnp.float32)
                    ref[(2 * c + h) * len(values) + y] = value.astype(jnp.bfloat16)

        for kind in (1, 2, 3):
            start_back(kind, c)

    @pl.loop(0, 8)
    def _(v):
        ref = square.at[pl.ds(2 * UNIT * v, 2 * UNIT)]
        pltpu.make_async_copy(ref, ref, back_recv.at[0, v]).wait()

    @pl.loop(0, 4)
    def _(v):
        for kind, ref in enumerate((own.at[v], above.at[v], below.at[v])):
            pltpu.make_async_copy(ref, ref, back_recv.at[kind + 1, v]).wait()

    def added(ref, at):
        value = ref[0, at].astype(jnp.float32)
        for v in range(1, 4):
            value += ref[v, at].astype(jnp.float32)
        return value

    @pl.loop(0, 8)
    def _(yy):
        under, over = added(below, yy), added(above, yy)
        for e in range(2):
            rims = jnp.concatenate([under[8 * e : 8 * e + 8], over[8 * e : 8 * e + 8]], axis=0)
            at = pl.multiple_of((2 * yy + e) * 16, 16)
            total[pl.ds(at, 16), :] = added(own, 2 * yy + e) + rims

    for x in range(16):
        grid[x] = total[pl.ds(x, 16, stride=16), :]

    @pl.loop(0, 4)
    def _(v):
        for item in plan:
            away, is_here = sends(v, *item)[3:]

            @pl.when(jnp.logical_not(is_here))
            def _():
                away.wait_send()

    def end_back(kind, c):
        away, is_here = goes_back(kind, c)[3:]

        @pl.when(jnp.logical_not(is_here))
        def _():
            away.wait_send()

    @pl.loop(0, COLS)
    def _(c):
        end_back(0, c)

    @pl.loop(0, COLS // 2)
    def _(w):
        for kind in range(3):
            share_parts(kind, 2 * w + 1 - core).wait_send()
            end_back(kind + 1, 2 * w + core)


def fused(pattern, anchors, blocks, basis_x, basis_yz):
    return pl.pallas_call(
        kernel,
        out_shape=[
            jax.ShapeDtypeStruct((64, B, B), jnp.bfloat16),
            jax.ShapeDtypeStruct((16, 16, 128), jnp.float32),
        ],
        in_specs=[ANY, ANY, ANY, VMEM, VMEM],
        out_specs=[ANY, VMEM],
        scratch_shapes=[pltpu.VMEM((HELD + 1, B, B), jnp.bfloat16)] * 5
        + [
            pltpu.VMEM((UNIT * K // 2, B, 2 * B), jnp.float32),
            pltpu.VMEM((HELD, B, B), jnp.bfloat16),
            pltpu.VMEM((K * 32, B), jnp.bfloat16),
            pltpu.VMEM((UNIT * K * SPAN, 32, 128), jnp.bfloat16),
            pltpu.VMEM((128, 16, 128), jnp.bfloat16),
            pltpu.VMEM((64, 16, 128), jnp.bfloat16),
            pltpu.VMEM((64, 16, 128), jnp.bfloat16),
            pltpu.VMEM((4, 16, 16, 128), jnp.bfloat16),
            pltpu.VMEM((4, 8, 16, 128), jnp.bfloat16),
            pltpu.VMEM((4, 8, 16, 128), jnp.bfloat16),
            pltpu.VMEM((256, 128), jnp.float32),
            pltpu.VMEM((4, 16, 16, 128), jnp.bfloat16),
            pltpu.VMEM((4, 8, 16, 128), jnp.bfloat16),
            pltpu.VMEM((4, 8, 16, 128), jnp.bfloat16),
            pltpu.VMEM((K, NBR), jnp.int32),
            pltpu.VMEM((3, K, NBR), jnp.int32),
            pltpu.VMEM((32, B), jnp.float32),
            pltpu.VMEM((B, 16 * B), jnp.bfloat16),
            pltpu.VMEM((TABLE, B), jnp.int32),
            pltpu.SMEM((TABLE, B), jnp.int32),
            pltpu.SemaphoreType.DMA((8, 3)),
            pltpu.SemaphoreType.DMA((3, COLS)),
            pltpu.SemaphoreType.DMA((2, COLS)),
            pltpu.SemaphoreType.DMA((2, COLS)),
            pltpu.SemaphoreType.DMA((4, COLS)),
            pltpu.SemaphoreType.DMA((4, 8)),
            pltpu.SemaphoreType.DMA((3, 4)),
            pltpu.SemaphoreType.DMA((3, 4)),
            pltpu.SemaphoreType.DMA((3,)),
        ],
        compiler_params=pltpu.CompilerParams(collective_id=0, has_side_effects=True, vmem_limit_bytes=60 << 20),
        name="square_and_tiles",
    )(pattern, anchors, blocks, basis_x, basis_yz)


def per_device(blocks, pattern, anchors, basis_x, basis_yz):
    square, grid = fused(pattern.T, jnp.transpose(anchors, (0, 2, 1)), blocks.reshape(64, B, B), basis_x, basis_yz)
    return square.reshape(32, 2, B, B).astype(jnp.float32), grid


def solution(mesh):
    placed = (P("row", "col", None, None), P(), P(), P(), P())
    return jax.shard_map(
        per_device,
        mesh=mesh,
        in_specs=placed,
        out_specs=(P("row", "col", None, None), P("row", "col", None)),
        check_vma=False,
    )
```
